32 devices in a mesh: groups: 2 (over y), tensor: 4 (over z), dp: 2 (over x), pipe: 2 (over core).
Axes of the slice: x: 2, y: 2, z: 4, core: 2. Of those that a mesh axis runs over, the one named last changes fastest.
Arguments:
- tokens: bfloat16 [4, 256, 4096], P(('groups', 'dp'), 'tensor'), parts along dimension 0, may hold values from -6 to 6
- gate_preactivation: bfloat16 [4, 14336, 256], P(('groups', 'dp'), ('tensor', 'pipe')), parts along dimension 0, may hold values from -6 to 6
- up_preactivation: bfloat16 [4, 14336, 256], P(('groups', 'dp'), ('tensor', 'pipe')), parts along dimension 0, may hold values from -6 to 6
- hidden_gradient: bfloat16 [4, 14336, 256], P(('groups', 'dp'), ('tensor', 'pipe')), parts along dimension 0, may hold values from -1 to 1
- gate_merged_weight: bfloat16 [14336, 4096], P(('tensor', 'pipe')), may hold values from -0.375 to 0.375
- up_merged_weight: bfloat16 [14336, 4096], P(('tensor', 'pipe')), may hold values from -0.375 to 0.375
- gate_down_factor: bfloat16 [64, 4096], P(None, 'pipe'), may hold values from -0.01171875 to 0.01171875
- up_down_factor: bfloat16 [64, 4096], P(None, 'pipe'), may hold values from -0.01171875 to 0.01171875
- gate_up_factor: bfloat16 [14336, 64], P(('tensor', 'pipe')), may hold values from -0.005859375 to 0.005859375
- up_up_factor: bfloat16 [14336, 64], P(('tensor', 'pipe')), may hold values from -0.005859375 to 0.005859375
Outputs:
- input_grad: bfloat16 [4, 256, 4096], P(('groups', 'dp'), ('tensor', 'pipe')), parts along dimension 0
- gate_a_grad: float32 [128, 4096], P('groups', 'pipe'), parts along dimension 0
- up_a_grad: float32 [128, 4096], P('groups', 'pipe'), parts along dimension 0
- gate_b_grad: float32 [28672, 64], P(('groups', 'tensor', 'pipe')), parts along dimension 0
- up_b_grad: float32 [28672, 64], P(('groups', 'tensor', 'pipe')), parts along dimension 0
The draws below stay inside these ranges and needn't reach their ends.
There are 2 independent parts, one for each index of `groups`. The reference program is written for one: setup_inputs(seed, part) draws one part's arguments, and reference() takes and returns one part's arrays. A program takes and returns all parts, laid end to end along the dimension named above; an argument that names none is the same for every part. Nothing has to cross between parts.
All inputs are finite; a program needn't handle non-finite values.
Results may differ from the reference program's by a relative error of at most 0.005.
Values may be sent and summed in bfloat16 or wider, within the bound.
A program may use at most 128 MiB of HBM per device.

```python
import jax
import jax.numpy as jnp
from jax import lax

MODEL_WIDTH = 4096
HIDDEN_UNITS = 14336
ADAPTER_RANK = 64
SEQ_LEN = 256
SEQS = 2
N_TENSOR = 4
N_PIPE = 2


def with_spikes(drawn, stream_key, source, target, blocks, factor):
    def block_of(position):
        return (jnp.arange(drawn.shape[position]) // (drawn.shape[position] // blocks)).reshape((-1,) + (1,) * (drawn.ndim - 1 - position))

    one_side = jax.random.permutation(stream_key, blocks)[block_of(target)]
    other_side = (block_of(target) + blocks // 2) % blocks
    return jnp.where((block_of(source) == one_side) | (block_of(source) == other_side), factor * drawn, drawn)


def levels(rng, shape, cuts, least, largest):
    gain = 1.0
    for position, blocks in cuts:
        heights = jax.random.uniform(jax.random.fold_in(jax.random.fold_in(rng, 6), position), (blocks,), jnp.float32, least / len(cuts), largest / len(cuts))
        gain = gain * jnp.repeat(jnp.exp(heights), shape[position] // blocks).reshape((-1,) + (1,) * (len(shape) - 1 - position))
    return gain


def scatter_about(rng, dims, scale, most, shards=(), held_as=jnp.bfloat16):
    drawn = jax.random.normal(rng, dims, jnp.float32) * scale
    if len(shards) > 0:
        drawn = levels(rng, dims, shards, -0.22, 0.18) * drawn
    return jnp.clip(drawn, min=-most, max=most).astype(held_as)


def noise_with(rng, extent, scale, most, shards, heavy, held_as=jnp.bfloat16):
    array = scale * jax.random.normal(rng, extent, jnp.float32)
    if shards:
        array = array * levels(rng, extent, shards, -0.22, 0.18)
    return jnp.clip(with_spikes(array, jax.random.fold_in(rng, 3), *heavy), -most, most).astype(held_as)


def setup_inputs(seed: int = 0, part: int = 0) -> dict:
    splits = jax.random.split(jax.random.key(seed), 11)
    part_keys = jax.random.split(jax.random.fold_in(splits[10], part), 11)
    return {
        "tokens": scatter_about(part_keys[0], (SEQS, SEQ_LEN, MODEL_WIDTH), 1.0, 6.0, ((0, 2), (1, 4))),
        "gate_preactivation": scatter_about(part_keys[1], (SEQS, HIDDEN_UNITS, SEQ_LEN), 1.0, 6.0, ((0, 2), (1, 8))),
        "up_preactivation": scatter_about(part_keys[2], (SEQS, HIDDEN_UNITS, SEQ_LEN), 1.0, 6.0, ((0, 2), (1, 8))),
        "hidden_gradient": noise_with(part_keys[3], (SEQS, HIDDEN_UNITS, SEQ_LEN), 0.125, 1.0, ((0, 2), (1, 8)), (1, 2, 8, 2.0)),
        "gate_merged_weight": scatter_about(splits[4], (HIDDEN_UNITS, MODEL_WIDTH), (HIDDEN_UNITS // 64) ** -0.5, 0.375, ((0, 8),)),
        "up_merged_weight": scatter_about(splits[5], (HIDDEN_UNITS, MODEL_WIDTH), (HIDDEN_UNITS // 64) ** -0.5, 0.375, ((0, 8),)),
        "gate_down_factor": scatter_about(splits[6], (ADAPTER_RANK, MODEL_WIDTH), (64 * MODEL_WIDTH) ** -0.5, 0.01171875, ((1, 2),)),
        "up_down_factor": scatter_about(splits[7], (ADAPTER_RANK, MODEL_WIDTH), (64 * MODEL_WIDTH) ** -0.5, 0.01171875, ((1, 2),)),
        "gate_up_factor": scatter_about(splits[8], (HIDDEN_UNITS, ADAPTER_RANK), (64 * HIDDEN_UNITS) ** -0.5, 0.005859375, ((0, 8),)),
        "up_up_factor": scatter_about(splits[9], (HIDDEN_UNITS, ADAPTER_RANK), (64 * HIDDEN_UNITS) ** -0.5, 0.005859375, ((0, 8),)),
    }


def reference(tokens, gate_preactivation, up_preactivation, hidden_gradient, gate_merged_weight, up_merged_weight, gate_down_factor, up_down_factor, gate_up_factor, up_up_factor):
    highest_precision = lax.Precision.HIGHEST
    gate_vals = gate_preactivation.astype(jnp.float32)
    up_vals = up_preactivation.astype(jnp.float32)
    grad_vals = hidden_gradient.astype(jnp.float32)
    sigmoid = jax.nn.sigmoid(gate_vals)
    gate_gradient = (grad_vals * up_vals * sigmoid * (1.0 + gate_vals * (1.0 - sigmoid))).astype(jnp.bfloat16)
    up_gradient = (grad_vals * gate_vals * sigmoid).astype(jnp.bfloat16)
    blocks = N_TENSOR * N_PIPE
    per_block = HIDDEN_UNITS // blocks
    gate_w_blocks = gate_merged_weight.reshape(blocks, per_block, MODEL_WIDTH)
    up_w_blocks = up_merged_weight.reshape(blocks, per_block, MODEL_WIDTH)

    def one_sequence(pair):
        gate_blocks = pair[0].reshape(blocks, per_block, SEQ_LEN)
        up_blocks = pair[1].reshape(blocks, per_block, SEQ_LEN)

        def add_block(total, parts):
            first = jnp.dot(parts[0].T, parts[2], preferred_element_type=jnp.float32)
            second = jnp.dot(parts[1].T, parts[3], preferred_element_type=jnp.float32)
            return total + (first + second), None

        start = jnp.zeros((SEQ_LEN, MODEL_WIDTH), jnp.float32)
        total, unused = lax.scan(add_block, start, (gate_blocks, up_blocks, gate_w_blocks, up_w_blocks))
        return total.astype(jnp.bfloat16)

    input_grad = lax.map(one_sequence, (gate_gradient, up_gradient))
    token_values = tokens.astype(jnp.float32)
    gate_full_width = gate_gradient.astype(jnp.float32)
    up_full_width = up_gradient.astype(jnp.float32)
    gate_projected = jnp.einsum("ghe,ae->gha", token_values, gate_down_factor.astype(jnp.float32), precision=highest_precision).astype(jnp.bfloat16)
    up_projected = jnp.einsum("ghe,ae->gha", token_values, up_down_factor.astype(jnp.float32), precision=highest_precision).astype(jnp.bfloat16)
    gate_b_grad = jnp.einsum("sft,stk->fk", gate_full_width, gate_projected.astype(jnp.float32), precision=highest_precision)
    up_b_grad = jnp.einsum("sft,stk->fk", up_full_width, up_projected.astype(jnp.float32), precision=highest_precision)
    gate_backward = jnp.einsum("wdp,do->wpo", gate_full_width, gate_up_factor.astype(jnp.float32), precision=highest_precision)
    up_backward = jnp.einsum("wdp,do->wpo", up_full_width, up_up_factor.astype(jnp.float32), precision=highest_precision)
    gate_a_grad = jnp.einsum("stk,std->kd", gate_backward, token_values, precision=highest_precision)
    up_a_grad = jnp.einsum("stk,std->kd", up_backward, token_values, precision=highest_precision)
    return (input_grad, gate_a_grad, up_a_grad, gate_b_grad, up_b_grad)
```

```python
import functools

import jax
import jax.numpy as jnp
from jax import lax
from jax.experimental import pallas as pl
from jax.experimental.pallas import tpu as pltpu
from jax.sharding import PartitionSpec as P

F32 = jnp.float32
BF16 = jnp.bfloat16
TILE = 512
SLOTS = 3


def remote(src, dst, send_sem, recv_sem, axis, index):
    return pltpu.make_async_remote_copy(
        src_ref=src,
        dst_ref=dst,
        send_sem=send_sem,
        recv_sem=recv_sem,
        device_id={axis: index},
        device_id_type=pl.DeviceIdType.MESH,
    )


def kernel(
    n,
    nd,
    tok,
    g,
    u,
    h,
    wg,
    wu,
    gd,
    ud,
    gu,
    uu,
    dx_out,
    ga_out,
    ua_out,
    gb_out,
    ub_out,
    grad_g,
    grad_u,
    trans_g,
    trans_u,
    wbuf,
    acc,
    pair_send,
    pair_recv,
    keep,
    z_send,
    z_recv,
    proj_pair,
    proj_all,
    back_pair,
    back_z,
    back_recv,
    b_all,
    ax_send,
    ax_recv,
    az_send,
    az_recv,
    a_all,
    w_sem,
    pair_ss,
    pair_rs,
    z_ss,
    z_rs,
    small_ss,
    small_rs,
    proj_ss,
    proj_rs,
    back_ss,
    back_rs,
    b_ss,
    b_rs,
    ax_ss,
    ax_rs,
    az_ss,
    az_rs,
    ag_ss,
    ag_rs,
    agx_ss,
    agx_rs,
):
    z = lax.axis_index("tensor")
    x = lax.axis_index("dp")
    c = lax.axis_index("pipe")
    other = 1 - c
    hidden, seq = g.shape
    width = wg.shape[1]
    tiles = width // TILE
    own = seq // (2 * n)
    half = gd.shape[1]
    rank = gd.shape[0]
    a_rows = 2 * rank // nd
    a_cols = half // n

    def weights(t, start):
        slot = lax.rem(t, SLOTS)
        columns = pl.ds(pl.multiple_of(t * TILE, TILE), TILE)
        for i, ref in enumerate((wg, wu)):
            copy = pltpu.make_async_copy(ref.at[:, columns], wbuf.at[slot, i], w_sem.at[slot, i])
            if start:
                copy.start()
            else:
                copy.wait()

    barrier = pltpu.get_barrier_semaphore()
    pl.semaphore_signal(
        barrier, inc=1, device_id={"pipe": other}, device_id_type=pl.DeviceIdType.MESH
    )
    for j in range(1, n):
        pl.semaphore_signal(
            barrier,
            inc=1,
            device_id={"tensor": lax.rem(z + j, n)},
            device_id_type=pl.DeviceIdType.MESH,
        )
    for j in range(1, nd):
        pl.semaphore_signal(
            barrier,
            inc=1,
            device_id={"dp": lax.rem(x + j, nd)},
            device_id_type=pl.DeviceIdType.MESH,
        )
    for t in range(SLOTS - 1):
        weights(t, True)

    tok_half = tok.at[:, pl.ds(pl.multiple_of(c * half, half), half)]
    down = jnp.concatenate([gd[...], ud[...]], axis=0)
    proj_pair[0] = lax.dot_general(
        tok_half[...], down, (((1,), (1,)), ((), ())), preferred_element_type=F32
    )
    pl.semaphore_wait(barrier, 1 + (n - 1) + (nd - 1))
    proj_copy = remote(
        proj_pair.at[0], proj_pair.at[1], small_ss.at[0], small_rs.at[0], "pipe", other
    )
    proj_copy.start()

    def activate(start, size):
        rows = pl.ds(start, size)
        gv = g[rows, :].astype(F32)
        uv = u[rows, :].astype(F32)
        hv = h[rows, :].astype(F32)
        s = jax.nn.sigmoid(gv)
        gg = (hv * uv * s * (1.0 + gv * (1.0 - s))).astype(BF16)
        ug = (hv * gv * s).astype(BF16)
        grad_g[rows, :] = gg
        grad_u[rows, :] = ug
        trans_g[:, rows] = gg.T
        trans_u[:, rows] = ug.T

    full = hidden // 128

    @pl.loop(0, full)
    def _(i):
        activate(pl.multiple_of(i * 128, 128), 128)

    if hidden % 128:
        activate(full * 128, hidden % 128)

    back_pair[0] = jnp.concatenate(
        [
            jnp.dot(trans_g[...], gu[...], preferred_element_type=F32),
            jnp.dot(trans_u[...], uu[...], preferred_element_type=F32),
        ],
        axis=1,
    )
    back_copy = remote(
        back_pair.at[0], back_pair.at[1], small_ss.at[1], small_rs.at[1], "pipe", other
    )
    back_copy.start()

    proj_copy.wait_recv()
    proj_all[z] = (proj_pair[0] + proj_pair[1]).astype(BF16)

    def proj_z(j):
        return remote(
            proj_all.at[z],
            proj_all.at[z],
            proj_ss.at[j - 1],
            proj_rs.at[j - 1],
            "tensor",
            lax.rem(z + j, n),
        )

    for j in range(1, n):
        proj_z(j).start()

    back_copy.wait_recv()
    back_z[...] = (back_pair[0] + back_pair[1]).reshape(back_z.shape)

    def back_to(j):
        to = lax.rem(z + j, n)
        return remote(
            back_z.at[to],
            back_recv.at[j - 1],
            back_ss.at[j - 1],
            back_rs.at[j - 1],
            "tensor",
            to,
        )

    for j in range(1, n):
        back_to(j).start()

    def b_to(j):
        return remote(
            b_all.at[x], b_all.at[x], b_ss.at[j - 1], b_rs.at[j - 1], "dp", lax.rem(x + j, nd)
        )

    def ax_to(j):
        to = lax.rem(x + j, nd)
        return remote(
            ax_send.at[to], ax_recv.at[j - 1], ax_ss.at[j - 1], ax_rs.at[j - 1], "dp", to
        )

    def az_to(j):
        to = lax.rem(z + j, n)
        return remote(
            az_send.at[to], az_recv.at[j - 1], az_ss.at[j - 1], az_rs.at[j - 1], "tensor", to
        )

    def ag_to(j):
        return remote(
            a_all.at[x, z],
            a_all.at[x, z],
            ag_ss.at[j - 1],
            ag_rs.at[j - 1],
            "tensor",
            lax.rem(z + j, n),
        )

    def agx_to(j):
        return remote(
            a_all.at[x], a_all.at[x], agx_ss.at[j - 1], agx_rs.at[j - 1], "dp", lax.rem(x + j, nd)
        )

    def a_partial():
        for j in range(1, n):
            back_to(j).wait_recv()
        total = back_z[z]
        for j in range(1, n):
            total = total + back_recv[j - 1]
        total = total.T
        high = total.astype(BF16)
        low = (total - high.astype(F32)).astype(BF16)
        part = jnp.dot(high, tok_half[...], preferred_element_type=F32)
        part = part + jnp.dot(low, tok_half[...], preferred_element_type=F32)
        for d in range(nd):
            ax_send[d] = part[d * a_rows : (d + 1) * a_rows].astype(BF16)
        for j in range(1, nd):
            ax_to(j).start()

    def b_partial():
        for j in range(1, n):
            proj_z(j).wait_recv()
        proj = proj_all[...].reshape(seq, 2 * rank)
        first = lax.broadcasted_iota(jnp.int32, proj.shape, 1) < rank
        zero = jnp.zeros_like(proj)
        part = jnp.dot(grad_g[...], jnp.where(first, proj, zero), preferred_element_type=F32)
        part = part + jnp.dot(grad_u[...], jnp.where(first, zero, proj), preferred_element_type=F32)
        b_all[x] = part.astype(BF16)
        for j in range(1, nd):
            b_to(j).start()

    def a_across():
        total = ax_send[x].astype(F32)
        for j in range(1, nd):
            ax_to(j).wait_recv()
        for j in range(1, nd):
            total = total + ax_recv[j - 1].astype(F32)
        for k in range(n):
            az_send[k] = total[:, k * a_cols : (k + 1) * a_cols].astype(BF16)
        for j in range(1, n):
            az_to(j).start()

    def a_along():
        total = az_send[z].astype(F32)
        for j in range(1, n):
            az_to(j).wait_recv()
        for j in range(1, n):
            total = total + az_recv[j - 1].astype(F32)
        a_all[x, z] = total.astype(BF16)
        for j in range(1, n):
            ag_to(j).start()

    def pair(t):
        return remote(
            pair_send.at[t], pair_recv.at[t], pair_ss.at[t], pair_rs.at[t], "pipe", other
        )

    def z_to(t, j):
        to = lax.rem(z + j, n)
        return remote(
            z_send.at[t, to], z_recv.at[t, j - 1], z_ss.at[t, j - 1], z_rs.at[t, j - 1], "tensor", to
        )

    def rows_of(k, core):
        return pl.ds(pl.multiple_of((2 * k + core) * own, own), own)

    def forward(t):
        slot = lax.rem(t, 2)
        pair(t).wait_recv()
        for k in range(n):
            z_send[t, k] = (acc[slot, rows_of(k, c), :] + pair_recv[t, k].astype(F32)).astype(BF16)
        for j in range(1, n):
            z_to(t, j).start()
        keep[t] = acc[slot, rows_of(z, c), :] + pair_recv[t, z].astype(F32)

    @pl.loop(0, tiles)
    def _(t):
        @pl.when(t + SLOTS - 1 < tiles)
        def _():
            weights(t + SLOTS - 1, True)

        weights(t, False)
        slot = lax.rem(t, 2)
        wslot = lax.rem(t, SLOTS)
        acc[slot] = jnp.dot(trans_g[...], wbuf[wslot, 0], preferred_element_type=F32) + jnp.dot(
            trans_u[...], wbuf[wslot, 1], preferred_element_type=F32
        )
        for k in range(n):
            pair_send[t, k] = acc[slot, rows_of(k, other), :].astype(BF16)
        pair(t).start()

        @pl.when(t > 0)
        def _():
            forward(t - 1)

        @pl.when(t == 1)
        def _():
            a_partial()

        @pl.when(t == 2)
        def _():
            b_partial()

        @pl.when(t == 4)
        def _():
            a_across()

        @pl.when(t == 6)
        def _():
            a_along()

    forward(tiles - 1)

    for j in range(1, n):
        ag_to(j).wait_recv()
    for j in range(1, nd):
        agx_to(j).start()

    for j in range(1, nd):
        b_to(j).wait_recv()
    total = b_all[0].astype(F32)
    for d in range(1, nd):
        total = total + b_all[d].astype(F32)
    gb_out[...] = total[:, :rank]
    ub_out[...] = total[:, rank:]

    @pl.loop(0, tiles)
    def _(t):
        total = keep[t]
        for j in range(1, n):
            z_to(t, j).wait_recv()
        for j in range(1, n):
            total = total + z_recv[t, j - 1].astype(F32)
        dx_out[:, pl.ds(pl.multiple_of(t * TILE, TILE), TILE)] = total.astype(BF16)
        pair(t).wait_send()
        for j in range(1, n):
            z_to(t, j).wait_send()

    for j in range(1, nd):
        agx_to(j).wait_recv()
    for d in range(nd):
        first = d * a_rows
        ref, row = (ga_out, first) if first < rank else (ua_out, first - rank)
        for k in range(n):
            ref[row : row + a_rows, k * a_cols : (k + 1) * a_cols] = a_all[d, k].astype(F32)

    proj_copy.wait_send()
    back_copy.wait_send()
    for j in range(1, n):
        proj_z(j).wait_send()
        back_to(j).wait_send()
        az_to(j).wait_send()
        ag_to(j).wait_send()
    for j in range(1, nd):
        b_to(j).wait_send()
        ax_to(j).wait_send()
        agx_to(j).wait_send()


def body(n, nd, tokens, gate, up, hidden_gradient, wg, wu, gd, ud, gu, uu):
    hidden, seq = gate.shape[1:]
    rows, width = tokens.shape[1:]
    rank, half = gd.shape
    tiles = width // TILE
    own = seq // (2 * n)
    a_rows = 2 * rank // nd
    a_cols = half // n
    dma = pltpu.SemaphoreType.DMA
    vmem = pl.BlockSpec(memory_space=pltpu.VMEM)
    hbm = pl.BlockSpec(memory_space=pl.ANY)
    outs = pl.pallas_call(
        functools.partial(kernel, n, nd),
        out_shape=(
            jax.ShapeDtypeStruct((own, width), BF16),
            jax.ShapeDtypeStruct((rank, half), F32),
            jax.ShapeDtypeStruct((rank, half), F32),
            jax.ShapeDtypeStruct((hidden, rank), F32),
            jax.ShapeDtypeStruct((hidden, rank), F32),
        ),
        in_specs=[vmem] * 4 + [hbm] * 2 + [vmem] * 4,
        out_specs=(vmem,) * 5,
        scratch_shapes=[
            pltpu.VMEM((hidden, seq), BF16),
            pltpu.VMEM((hidden, seq), BF16),
            pltpu.VMEM((seq, hidden), BF16),
            pltpu.VMEM((seq, hidden), BF16),
            pltpu.VMEM((SLOTS, 2, hidden, TILE), BF16),
            pltpu.VMEM((2, seq, TILE), F32),
            pltpu.VMEM((tiles, n, own, TILE), BF16),
            pltpu.VMEM((tiles, n, own, TILE), BF16),
            pltpu.VMEM((tiles, own, TILE), F32),
            pltpu.VMEM((tiles, n, own, TILE), BF16),
            pltpu.VMEM((tiles, n - 1, own, TILE), BF16),
            pltpu.VMEM((2, rows, 2 * rank), F32),
            pltpu.VMEM((n, rows, 2 * rank), BF16),
            pltpu.VMEM((2, seq, 2 * rank), F32),
            pltpu.VMEM((n, rows, 2 * rank), F32),
            pltpu.VMEM((n - 1, rows, 2 * rank), F32),
            pltpu.VMEM((nd, hidden, 2 * rank), BF16),
            pltpu.VMEM((nd, a_rows, half), BF16),
            pltpu.VMEM((nd - 1, a_rows, half), BF16),
            pltpu.VMEM((n, a_rows, a_cols), BF16),
            pltpu.VMEM((n - 1, a_rows, a_cols), BF16),
            pltpu.VMEM((nd, n, a_rows, a_cols), BF16),
            dma((SLOTS, 2)),
            dma((tiles,)),
            dma((tiles,)),
            dma((tiles, n - 1)),
            dma((tiles, n - 1)),
            dma((2,)),
            dma((2,)),
            dma((n - 1,)),
            dma((n - 1,)),
            dma((n - 1,)),
            dma((n - 1,)),
            dma((nd - 1,)),
            dma((nd - 1,)),
            dma((nd - 1,)),
            dma((nd - 1,)),
            dma((n - 1,)),
            dma((n - 1,)),
            dma((n - 1,)),
            dma((n - 1,)),
            dma((nd - 1,)),
            dma((nd - 1,)),
        ],
        compiler_params=pltpu.CompilerParams(
            collective_id=0, has_side_effects=True, vmem_limit_bytes=56 * 1024 * 1024
        ),
        cost_estimate=pl.CostEstimate(
            flops=4 * seq * hidden * width, bytes_accessed=4 * hidden * width, transcendentals=0
        ),
    )(tokens[0], gate[0], up[0], hidden_gradient[0], wg, wu, gd, ud, gu, uu)
    return (outs[0][None],) + tuple(outs[1:])


def solution(mesh):
    placed = (
        P(("groups", "dp"), "tensor", None),
        P(("groups", "dp"), ("tensor", "pipe"), None),
        P(("groups", "dp"), ("tensor", "pipe"), None),
        P(("groups", "dp"), ("tensor", "pipe"), None),
        P(("tensor", "pipe"), None),
        P(("tensor", "pipe"), None),
        P(None, "pipe"),
        P(None, "pipe"),
        P(("tensor", "pipe"), None),
        P(("tensor", "pipe"), None),
    )
    return jax.shard_map(
        functools.partial(body, mesh.shape["tensor"], mesh.shape["dp"]),
        mesh=mesh,
        in_specs=placed,
        out_specs=(
            P(("groups", "dp"), ("tensor", "pipe"), None),
            P("groups", "pipe"),
            P("groups", "pipe"),
            P(("groups", "tensor", "pipe"), None),
            P(("groups", "tensor", "pipe"), None),
        ),
        check_vma=False,
    )
```

```python
import functools

import jax
import jax.numpy as jnp
from jax import lax
from jax.experimental import pallas as pl
from jax.experimental.pallas import tpu as pltpu
from jax.sharding import PartitionSpec as P

F32 = jnp.float32
BF16 = jnp.bfloat16
TILE = 512
SLOTS = 3


def remote(src, dst, send_sem, recv_sem, axis, index):
    return pltpu.make_async_remote_copy(
        src_ref=src,
        dst_ref=dst,
        send_sem=send_sem,
        recv_sem=recv_sem,
        device_id={axis: index},
        device_id_type=pl.DeviceIdType.MESH,
    )


def kernel(
    n,
    nd,
    tok,
    g_hbm,
    u_hbm,
    h_hbm,
    wg,
    wu,
    gd,
    ud,
    gu,
    uu,
    dx_out,
    a_out,
    b_out,
    g,
    u,
    h,
    trans_g,
    trans_u,
    wbuf,
    acc,
    pair_send,
    pair_recv,
    keep,
    z_send,
    z_recv,
    proj_pair,
    proj_all,
    back_pair,
    back_z,
    back_recv,
    b_all,
    ax_send,
    ax_recv,
    az_send,
    az_recv,
    a_all,
    w_sem,
    pair_ss,
    pair_rs,
    z_ss,
    z_rs,
    small_ss,
    small_rs,
    proj_ss,
    proj_rs,
    back_ss,
    back_rs,
    b_ss,
    b_rs,
    ax_ss,
    ax_rs,
    az_ss,
    az_rs,
    ag_ss,
    ag_rs,
    agx_ss,
    agx_rs,
    in_sem,
    out_sem,
):
    z = lax.axis_index("tensor")
    x = lax.axis_index("dp")
    c = lax.axis_index("pipe")
    other = 1 - c
    hidden, seq = g.shape
    width = wg.shape[1]
    tiles = width // TILE
    own = seq // (2 * n)
    half = gd.shape[1]
    rank = gd.shape[0]
    a_rows = 2 * rank // nd
    a_cols = half // n

    def weights(t, start):
        slot = lax.rem(t, SLOTS)
        columns = pl.ds(pl.multiple_of(t * TILE, TILE), TILE)
        for i, ref in enumerate((wg, wu)):
            copy = pltpu.make_async_copy(ref.at[:, columns], wbuf.at[slot, i], w_sem.at[slot, i])
            if start:
                copy.start()
            else:
                copy.wait()

    barrier = pltpu.get_barrier_semaphore()
    pl.semaphore_signal(
        barrier, inc=1, device_id={"pipe": other}, device_id_type=pl.DeviceIdType.MESH
    )
    for j in range(1, n):
        pl.semaphore_signal(
            barrier,
            inc=1,
            device_id={"tensor": lax.rem(z + j, n)},
            device_id_type=pl.DeviceIdType.MESH,
        )
    for j in range(1, nd):
        pl.semaphore_signal(
            barrier,
            inc=1,
            device_id={"dp": lax.rem(x + j, nd)},
            device_id_type=pl.DeviceIdType.MESH,
        )
    loads = [
        pltpu.make_async_copy(src, dst, in_sem.at[i])
        for i, (src, dst) in enumerate(((g_hbm, g), (u_hbm, u), (h_hbm, h)))
    ]
    for load in loads:
        load.start()
    for t in range(SLOTS - 1):
        weights(t, True)

    tok_half = tok.at[:, pl.ds(pl.multiple_of(c * half, half), half)]
    down = jnp.concatenate([gd[...], ud[...]], axis=0)
    proj_pair[0] = lax.dot_general(
        tok_half[...], down, (((1,), (1,)), ((), ())), preferred_element_type=F32
    )
    pl.semaphore_wait(barrier, 1 + (n - 1) + (nd - 1))
    proj_copy = remote(
        proj_pair.at[0], proj_pair.at[1], small_ss.at[0], small_rs.at[0], "pipe", other
    )
    proj_copy.start()

    def activate(start, size):
        rows = pl.ds(start, size)
        gv = g[rows, :].astype(F32)
        uv = u[rows, :].astype(F32)
        hv = h[rows, :].astype(F32)
        s = jax.nn.sigmoid(gv)
        gg = (hv * uv * s * (1.0 + gv * (1.0 - s))).astype(BF16)
        ug = (hv * gv * s).astype(BF16)
        trans_g[:, rows] = gg.T
        trans_u[:, rows] = ug.T

    for load in loads:
        load.wait()
    full = hidden // 128

    @pl.loop(0, full)
    def _(i):
        activate(pl.multiple_of(i * 128, 128), 128)

    if hidden % 128:
        activate(full * 128, hidden % 128)

    back_pair[0] = jnp.concatenate(
        [
            lax.dot_general(
                trans_g[...], gu[...], (((1,), (1,)), ((), ())), preferred_element_type=F32
            ),
            lax.dot_general(
                trans_u[...], uu[...], (((1,), (1,)), ((), ())), preferred_element_type=F32
            ),
        ],
        axis=1,
    )
    back_copy = remote(
        back_pair.at[0], back_pair.at[1], small_ss.at[1], small_rs.at[1], "pipe", other
    )
    back_copy.start()

    proj_copy.wait_recv()
    proj_all[z] = (proj_pair[0] + proj_pair[1]).astype(BF16)

    def proj_z(j):
        return remote(
            proj_all.at[z],
            proj_all.at[z],
            proj_ss.at[j - 1],
            proj_rs.at[j - 1],
            "tensor",
            lax.rem(z + j, n),
        )

    for j in range(1, n):
        proj_z(j).start()

    back_copy.wait_recv()
    back_z[...] = (back_pair[0] + back_pair[1]).reshape(back_z.shape)

    def back_to(j):
        to = lax.rem(z + j, n)
        return remote(
            back_z.at[to],
            back_recv.at[j - 1],
            back_ss.at[j - 1],
            back_rs.at[j - 1],
            "tensor",
            to,
        )

    for j in range(1, n):
        back_to(j).start()

    def b_to(j):
        return remote(
            b_all.at[x], b_all.at[x], b_ss.at[j - 1], b_rs.at[j - 1], "dp", lax.rem(x + j, nd)
        )

    def ax_to(j):
        to = lax.rem(x + j, nd)
        return remote(
            ax_send.at[to], ax_recv.at[j - 1], ax_ss.at[j - 1], ax_rs.at[j - 1], "dp", to
        )

    def az_to(j):
        to = lax.rem(z + j, n)
        return remote(
            az_send.at[to], az_recv.at[j - 1], az_ss.at[j - 1], az_rs.at[j - 1], "tensor", to
        )

    def ag_to(j):
        return remote(
            a_all.at[x, z],
            a_all.at[x, z],
            ag_ss.at[j - 1],
            ag_rs.at[j - 1],
            "tensor",
            lax.rem(z + j, n),
        )

    def agx_to(j):
        return remote(
            a_all.at[x], a_all.at[x], agx_ss.at[j - 1], agx_rs.at[j - 1], "dp", lax.rem(x + j, nd)
        )

    def a_partial():
        for j in range(1, n):
            back_to(j).wait_recv()
        total = back_z[z]
        for j in range(1, n):
            total = total + back_recv[j - 1]
        total = total.T
        high = total.astype(BF16)
        low = (total - high.astype(F32)).astype(BF16)
        part = jnp.dot(high, tok_half[...], preferred_element_type=F32)
        part = part + jnp.dot(low, tok_half[...], preferred_element_type=F32)
        for d in range(nd):
            ax_send[d] = part[d * a_rows : (d + 1) * a_rows].astype(BF16)
        for j in range(1, nd):
            ax_to(j).start()

    def b_partial():
        for j in range(1, n):
            proj_z(j).wait_recv()
        proj = proj_all[...].reshape(seq, 2 * rank).T
        for i, ref in enumerate((trans_g, trans_u)):
            rows = slice(i * rank, (i + 1) * rank)
            b_all[x, rows, :] = jnp.dot(
                proj[rows], ref[...], preferred_element_type=F32
            ).astype(BF16)
        for j in range(1, nd):
            b_to(j).start()

    def a_across():
        total = ax_send[x].astype(F32)
        for j in range(1, nd):
            ax_to(j).wait_recv()
        for j in range(1, nd):
            total = total + ax_recv[j - 1].astype(F32)
        for k in range(n):
            az_send[k] = total[:, k * a_cols : (k + 1) * a_cols].astype(BF16)
        for j in range(1, n):
            az_to(j).start()

    def a_along():
        total = az_send[z].astype(F32)
        for j in range(1, n):
            az_to(j).wait_recv()
        for j in range(1, n):
            total = total + az_recv[j - 1].astype(F32)
        a_all[x, z] = total.astype(BF16)
        for j in range(1, n):
            ag_to(j).start()

    def pair(t):
        return remote(
            pair_send.at[t], pair_recv.at[t], pair_ss.at[t], pair_rs.at[t], "pipe", other
        )

    def z_to(t, j):
        to = lax.rem(z + j, n)
        return remote(
            z_send.at[t, to], z_recv.at[t, j - 1], z_ss.at[t, j - 1], z_rs.at[t, j - 1], "tensor", to
        )

    def rows_of(k, core):
        return pl.ds(pl.multiple_of((2 * k + core) * own, own), own)

    def forward(t):
        slot = lax.rem(t, 2)
        pair(t).wait_recv()
        for k in range(n):
            z_send[t, k] = (acc[slot, rows_of(k, c), :] + pair_recv[t, k].astype(F32)).astype(BF16)
        for j in range(1, n):
            z_to(t, j).start()
        keep[t] = acc[slot, rows_of(z, c), :] + pair_recv[t, z].astype(F32)

    @pl.loop(0, tiles)
    def _(t):
        @pl.when(t + SLOTS - 1 < tiles)
        def _():
            weights(t + SLOTS - 1, True)

        weights(t, False)
        slot = lax.rem(t, 2)
        wslot = lax.rem(t, SLOTS)
        acc[slot] = jnp.dot(trans_g[...], wbuf[wslot, 0], preferred_element_type=F32) + jnp.dot(
            trans_u[...], wbuf[wslot, 1], preferred_element_type=F32
        )
        for k in range(n):
            pair_send[t, k] = acc[slot, rows_of(k, other), :].astype(BF16)
        pair(t).start()

        @pl.when(t > 0)
        def _():
            forward(t - 1)

        @pl.when(t == 0)
        def _():
            a_partial()

        @pl.when(t == 1)
        def _():
            b_partial()

        @pl.when(t == 3)
        def _():
            a_across()

        @pl.when(t == 5)
        def _():
            a_along()

    forward(tiles - 1)

    for j in range(1, n):
        ag_to(j).wait_recv()
    for j in range(1, nd):
        agx_to(j).start()

    for j in range(1, nd):
        b_to(j).wait_recv()
    b_store = pltpu.make_async_copy(b_all, b_out, out_sem.at[0])
    b_store.start()

    @pl.loop(0, tiles)
    def _(t):
        total = keep[t]
        for j in range(1, n):
            z_to(t, j).wait_recv()
        for j in range(1, n):
            total = total + z_recv[t, j - 1].astype(F32)
        dx_out[:, pl.ds(pl.multiple_of(t * TILE, TILE), TILE)] = total.astype(BF16)
        pair(t).wait_send()
        for j in range(1, n):
            z_to(t, j).wait_send()

    for j in range(1, nd):
        agx_to(j).wait_recv()
    a_store = pltpu.make_async_copy(a_all, a_out, out_sem.at[1])
    a_store.start()
    a_store.wait()
    b_store.wait()

    proj_copy.wait_send()
    back_copy.wait_send()
    for j in range(1, n):
        proj_z(j).wait_send()
        back_to(j).wait_send()
        az_to(j).wait_send()
        ag_to(j).wait_send()
    for j in range(1, nd):
        b_to(j).wait_send()
        ax_to(j).wait_send()
        agx_to(j).wait_send()


def finish(dx, a_all, b_all, dx_out, ga_out, ua_out, gb_out, ub_out):
    nd, n, a_rows, a_cols = a_all.shape
    rank = ga_out.shape[0]
    dx_out[...] = dx[...]
    for d in range(nd):
        first = d * a_rows
        ref, row = (ga_out, first) if first < rank else (ua_out, first - rank)
        for k in range(n):
            ref[row : row + a_rows, k * a_cols : (k + 1) * a_cols] = a_all[d, k].astype(F32)
    for i, ref in enumerate((gb_out, ub_out)):
        rows = slice(i * rank, (i + 1) * rank)
        total = b_all[0, rows, :].astype(F32)
        for d in range(1, nd):
            total = total + b_all[d, rows, :].astype(F32)
        ref[...] = total


def body(n, nd, tokens, gate, up, hidden_gradient, wg, wu, gd, ud, gu, uu):
    hidden, seq = gate.shape[1:]
    rows, width = tokens.shape[1:]
    rank, half = gd.shape
    tiles = width // TILE
    own = seq // (2 * n)
    a_rows = 2 * rank // nd
    a_cols = half // n
    dma = pltpu.SemaphoreType.DMA
    vmem = pl.BlockSpec(memory_space=pltpu.VMEM)
    hbm = pl.BlockSpec(memory_space=pl.ANY)
    outs = pl.pallas_call(
        functools.partial(kernel, n, nd),
        out_shape=(
            jax.ShapeDtypeStruct((own, width), BF16),
            jax.ShapeDtypeStruct((nd, n, a_rows, a_cols), BF16),
            jax.ShapeDtypeStruct((nd, 2 * rank, hidden), BF16),
        ),
        in_specs=[vmem] + [hbm] * 5 + [vmem] * 4,
        out_specs=(vmem, hbm, hbm),
        scratch_shapes=[
            pltpu.VMEM((hidden, seq), BF16),
            pltpu.VMEM((hidden, seq), BF16),
            pltpu.VMEM((hidden, seq), BF16),
            pltpu.VMEM((seq, hidden), BF16),
            pltpu.VMEM((seq, hidden), BF16),
            pltpu.VMEM((SLOTS, 2, hidden, TILE), BF16),
            pltpu.VMEM((2, seq, TILE), F32),
            pltpu.VMEM((tiles, n, own, TILE), BF16),
            pltpu.VMEM((tiles, n, own, TILE), BF16),
            pltpu.VMEM((tiles, own, TILE), F32),
            pltpu.VMEM((tiles, n, own, TILE), BF16),
            pltpu.VMEM((tiles, n - 1, own, TILE), BF16),
            pltpu.VMEM((2, rows, 2 * rank), F32),
            pltpu.VMEM((n, rows, 2 * rank), BF16),
            pltpu.VMEM((2, seq, 2 * rank), F32),
            pltpu.VMEM((n, rows, 2 * rank), F32),
            pltpu.VMEM((n - 1, rows, 2 * rank), F32),
            pltpu.VMEM((nd, 2 * rank, hidden), BF16),
            pltpu.VMEM((nd, a_rows, half), BF16),
            pltpu.VMEM((nd - 1, a_rows, half), BF16),
            pltpu.VMEM((n, a_rows, a_cols), BF16),
            pltpu.VMEM((n - 1, a_rows, a_cols), BF16),
            pltpu.VMEM((nd, n, a_rows, a_cols), BF16),
            dma((SLOTS, 2)),
            dma((tiles,)),
            dma((tiles,)),
            dma((tiles, n - 1)),
            dma((tiles, n - 1)),
            dma((2,)),
            dma((2,)),
            dma((n - 1,)),
            dma((n - 1,)),
            dma((n - 1,)),
            dma((n - 1,)),
            dma((nd - 1,)),
            dma((nd - 1,)),
            dma((nd - 1,)),
            dma((nd - 1,)),
            dma((n - 1,)),
            dma((n - 1,)),
            dma((n - 1,)),
            dma((n - 1,)),
            dma((nd - 1,)),
            dma((nd - 1,)),
            dma((3,)),
            dma((2,)),
        ],
        compiler_params=pltpu.CompilerParams(
            collective_id=0, has_side_effects=True, vmem_limit_bytes=56 * 1024 * 1024
        ),
        cost_estimate=pl.CostEstimate(
            flops=4 * seq * hidden * width, bytes_accessed=4 * hidden * width, transcendentals=0
        ),
    )(tokens[0], gate[0], up[0], hidden_gradient[0], wg, wu, gd, ud, gu.T, uu.T)
    dx, ga, ua, gb, ub = pl.pallas_call(
        finish,
        out_shape=(
            jax.ShapeDtypeStruct((own, width), BF16),
            jax.ShapeDtypeStruct((rank, half), F32),
            jax.ShapeDtypeStruct((rank, half), F32),
            jax.ShapeDtypeStruct((rank, hidden), F32),
            jax.ShapeDtypeStruct((rank, hidden), F32),
        ),
        in_specs=[vmem] * 3,
        out_specs=(vmem,) * 5,
        compiler_params=pltpu.CompilerParams(vmem_limit_bytes=32 * 1024 * 1024),
    )(*outs)
    return dx[None], ga, ua, gb.T, ub.T


def solution(mesh):
    placed = (
        P(("groups", "dp"), "tensor", None),
        P(("groups", "dp"), ("tensor", "pipe"), None),
        P(("groups", "dp"), ("tensor", "pipe"), None),
        P(("groups", "dp"), ("tensor", "pipe"), None),
        P(("tensor", "pipe"), None),
        P(("tensor", "pipe"), None),
        P(None, "pipe"),
        P(None, "pipe"),
        P(("tensor", "pipe"), None),
        P(("tensor", "pipe"), None),
    )
    return jax.shard_map(
        functools.partial(body, mesh.shape["tensor"], mesh.shape["dp"]),
        mesh=mesh,
        in_specs=placed,
        out_specs=(
            P(("groups", "dp"), ("tensor", "pipe"), None),
            P("groups", "pipe"),
            P("groups", "pipe"),
            P(("groups", "tensor", "pipe"), None),
            P(("groups", "tensor", "pipe"), None),
        ),
        check_vma=False,
    )
```

```python
import functools

import jax
import jax.numpy as jnp
from jax import lax
from jax.experimental import pallas as pl
from jax.experimental.pallas import tpu as pltpu
from jax.sharding import PartitionSpec as P

F32 = jnp.float32
BF16 = jnp.bfloat16
TILE = 512
SLOTS = 3


def remote(src, dst, send_sem, recv_sem, axis, index):
    return pltpu.make_async_remote_copy(
        src_ref=src,
        dst_ref=dst,
        send_sem=send_sem,
        recv_sem=recv_sem,
        device_id={axis: index},
        device_id_type=pl.DeviceIdType.MESH,
    )


def kernel(
    n,
    nd,
    tok,
    g_hbm,
    u_hbm,
    h_hbm,
    wg,
    wu,
    gd,
    ud,
    gu,
    uu,
    dx_out,
    a_out,
    b_out,
    g,
    u,
    h,
    trans_g,
    trans_u,
    wbuf,
    acc,
    pair_send,
    pair_recv,
    sums,
    z_send,
    from_below,
    from_above,
    proj_pair,
    proj_all,
    back_pair,
    back_z,
    back_recv,
    b_all,
    ax_send,
    ax_recv,
    az_send,
    az_recv,
    a_all,
    w_sem,
    pair_ss,
    pair_rs,
    z_ss,
    below_rs,
    above_rs,
    small_ss,
    small_rs,
    proj_ss,
    proj_rs,
    back_ss,
    back_rs,
    b_ss,
    b_rs,
    ax_ss,
    ax_rs,
    az_ss,
    az_rs,
    ag_ss,
    ag_rs,
    agx_ss,
    agx_rs,
    in_sem,
    out_sem,
):
    z = lax.axis_index("tensor")
    x = lax.axis_index("dp")
    c = lax.axis_index("pipe")
    other = 1 - c
    hidden, seq = g.shape
    width = wg.shape[1]
    tiles = width // TILE
    own = seq // (2 * n)
    half = gd.shape[1]
    rank = gd.shape[0]
    a_rows = 2 * rank // nd
    a_cols = half // n

    def weights(t, start):
        slot = lax.rem(t, SLOTS)
        columns = pl.ds(pl.multiple_of(t * TILE, TILE), TILE)
        for i, ref in enumerate((wg, wu)):
            copy = pltpu.make_async_copy(ref.at[:, columns], wbuf.at[slot, i], w_sem.at[slot, i])
            if start:
                copy.start()
            else:
                copy.wait()

    barrier = pltpu.get_barrier_semaphore()
    pl.semaphore_signal(
        barrier, inc=1, device_id={"pipe": other}, device_id_type=pl.DeviceIdType.MESH
    )
    for j in range(1, n):
        pl.semaphore_signal(
            barrier,
            inc=1,
            device_id={"tensor": lax.rem(z + j, n)},
            device_id_type=pl.DeviceIdType.MESH,
        )
    for j in range(1, nd):
        pl.semaphore_signal(
            barrier,
            inc=1,
            device_id={"dp": lax.rem(x + j, nd)},
            device_id_type=pl.DeviceIdType.MESH,
        )
    loads = [
        pltpu.make_async_copy(src, dst, in_sem.at[i])
        for i, (src, dst) in enumerate(((g_hbm, g), (u_hbm, u), (h_hbm, h)))
    ]
    for load in loads:
        load.start()
    for t in range(SLOTS - 1):
        weights(t, True)

    tok_half = tok.at[:, pl.ds(pl.multiple_of(c * half, half), half)]
    down = jnp.concatenate([gd[...], ud[...]], axis=0)
    proj_pair[0] = lax.dot_general(
        tok_half[...], down, (((1,), (1,)), ((), ())), preferred_element_type=F32
    )
    pl.semaphore_wait(barrier, 1 + (n - 1) + (nd - 1))
    proj_copy = remote(
        proj_pair.at[0], proj_pair.at[1], small_ss.at[0], small_rs.at[0], "pipe", other
    )
    proj_copy.start()

    def activate(start, size):
        rows = pl.ds(start, size)
        gv = g[rows, :].astype(F32)
        uv = u[rows, :].astype(F32)
        hv = h[rows, :].astype(F32)
        s = jax.nn.sigmoid(gv)
        gg = (hv * uv * s * (1.0 + gv * (1.0 - s))).astype(BF16)
        ug = (hv * gv * s).astype(BF16)
        trans_g[:, rows] = gg.T
        trans_u[:, rows] = ug.T

    for load in loads:
        load.wait()
    full = hidden // 128

    @pl.loop(0, full)
    def _(i):
        activate(pl.multiple_of(i * 128, 128), 128)

    if hidden % 128:
        activate(full * 128, hidden % 128)

    back_pair[0] = jnp.concatenate(
        [
            lax.dot_general(
                trans_g[...], gu[...], (((1,), (1,)), ((), ())), preferred_element_type=F32
            ),
            lax.dot_general(
                trans_u[...], uu[...], (((1,), (1,)), ((), ())), preferred_element_type=F32
            ),
        ],
        axis=1,
    )
    back_copy = remote(
        back_pair.at[0], back_pair.at[1], small_ss.at[1], small_rs.at[1], "pipe", other
    )
    back_copy.start()

    proj_copy.wait_recv()
    proj_all[z] = (proj_pair[0] + proj_pair[1]).astype(BF16)

    def proj_z(j):
        return remote(
            proj_all.at[z],
            proj_all.at[z],
            proj_ss.at[j - 1],
            proj_rs.at[j - 1],
            "tensor",
            lax.rem(z + j, n),
        )

    for j in range(1, n):
        proj_z(j).start()

    back_copy.wait_recv()
    back_z[...] = (back_pair[0] + back_pair[1]).reshape(back_z.shape)

    def back_to(j):
        to = lax.rem(z + j, n)
        return remote(
            back_z.at[to],
            back_recv.at[j - 1],
            back_ss.at[j - 1],
            back_rs.at[j - 1],
            "tensor",
            to,
        )

    for j in range(1, n):
        back_to(j).start()

    def b_to(j):
        return remote(
            b_all.at[x], b_all.at[x], b_ss.at[j - 1], b_rs.at[j - 1], "dp", lax.rem(x + j, nd)
        )

    def ax_to(j):
        to = lax.rem(x + j, nd)
        return remote(
            ax_send.at[to], ax_recv.at[j - 1], ax_ss.at[j - 1], ax_rs.at[j - 1], "dp", to
        )

    def az_to(j):
        to = lax.rem(z + j, n)
        return remote(
            az_send.at[to], az_recv.at[j - 1], az_ss.at[j - 1], az_rs.at[j - 1], "tensor", to
        )

    def ag_to(j):
        return remote(
            a_all.at[x, z],
            a_all.at[x, z],
            ag_ss.at[j - 1],
            ag_rs.at[j - 1],
            "tensor",
            lax.rem(z + j, n),
        )

    def agx_to(j):
        return remote(
            a_all.at[x], a_all.at[x], agx_ss.at[j - 1], agx_rs.at[j - 1], "dp", lax.rem(x + j, nd)
        )

    def a_partial():
        for j in range(1, n):
            back_to(j).wait_recv()
        total = back_z[z]
        for j in range(1, n):
            total = total + back_recv[j - 1]
        total = total.T
        high = total.astype(BF16)
        low = (total - high.astype(F32)).astype(BF16)
        part = jnp.dot(high, tok_half[...], preferred_element_type=F32)
        part = part + jnp.dot(low, tok_half[...], preferred_element_type=F32)
        for d in range(nd):
            ax_send[d] = part[d * a_rows : (d + 1) * a_rows].astype(BF16)
        for j in range(1, nd):
            ax_to(j).start()

    def b_partial():
        for j in range(1, n):
            proj_z(j).wait_recv()
        proj = proj_all[...].reshape(seq, 2 * rank).T
        for i, ref in enumerate((trans_g, trans_u)):
            rows = slice(i * rank, (i + 1) * rank)
            b_all[x, rows, :] = jnp.dot(
                proj[rows], ref[...], preferred_element_type=F32
            ).astype(BF16)
        for j in range(1, nd):
            b_to(j).start()

    def a_across():
        total = ax_send[x].astype(F32)
        for j in range(1, nd):
            ax_to(j).wait_recv()
        for j in range(1, nd):
            total = total + ax_recv[j - 1].astype(F32)
        for k in range(n):
            az_send[k] = total[:, k * a_cols : (k + 1) * a_cols].astype(BF16)
        for j in range(1, n):
            az_to(j).start()

    def a_along():
        total = az_send[z].astype(F32)
        for j in range(1, n):
            az_to(j).wait_recv()
        for j in range(1, n):
            total = total + az_recv[j - 1].astype(F32)
        a_all[x, z] = total.astype(BF16)
        for j in range(1, n):
            ag_to(j).start()

    def pair(t):
        return remote(
            pair_send.at[t], pair_recv.at[t], pair_ss.at[t], pair_rs.at[t], "pipe", other
        )

    def up_to(t, k):
        return remote(
            z_send.at[t, k], from_below.at[t, k], z_ss.at[t, k], below_rs.at[t, k], "tensor", lax.rem(z + 1, n)
        )

    def down_to(t, k):
        return remote(
            z_send.at[t, k], from_above.at[t, k], z_ss.at[t, k], above_rs.at[t, k], "tensor", lax.rem(z + n - 1, n)
        )

    def climb(t):
        for k in range(1, n):

            @pl.when(k > z)
            def _():
                @pl.when(z > 0)
                def _():
                    up_to(t, k).wait_recv()
                    z_send[t, k] = (sums[t, k] + from_below[t, k].astype(F32)).astype(BF16)

                @pl.when(z == 0)
                def _():
                    z_send[t, k] = sums[t, k].astype(BF16)

                up_to(t, k).start()

    def descend(t):
        for k in range(n - 1):

            @pl.when(k < z)
            def _():
                @pl.when(z < n - 1)
                def _():
                    down_to(t, k).wait_recv()
                    z_send[t, k] = (sums[t, k] + from_above[t, k].astype(F32)).astype(BF16)

                @pl.when(z == n - 1)
                def _():
                    z_send[t, k] = sums[t, k].astype(BF16)

                down_to(t, k).start()

    def rows_of(k, core):
        return pl.ds(pl.multiple_of((2 * k + core) * own, own), own)

    def forward(t):
        slot = lax.rem(t, 2)
        pair(t).wait_recv()
        for k in range(n):
            sums[t, k] = acc[slot, rows_of(k, c), :] + pair_recv[t, k].astype(F32)

    def multiply(t):
        @pl.when(t + SLOTS - 1 < tiles)
        def _():
            weights(t + SLOTS - 1, True)

        weights(t, False)
        slot = lax.rem(t, 2)
        wslot = lax.rem(t, SLOTS)
        acc[slot] = jnp.dot(trans_g[...], wbuf[wslot, 0], preferred_element_type=F32) + jnp.dot(
            trans_u[...], wbuf[wslot, 1], preferred_element_type=F32
        )
        for k in range(n):
            pair_send[t, k] = acc[slot, rows_of(k, other), :].astype(BF16)
        pair(t).start()

    @pl.loop(0, tiles + n - 1)
    def _(t):
        @pl.when(t < tiles)
        def _():
            multiply(t)

        @pl.when((t > 0) & (t <= tiles))
        def _():
            forward(t - 1)

        rising = t - 1 - z
        falling = t - n + z

        @pl.when((rising >= 0) & (rising < tiles))
        def _():
            climb(rising)

        @pl.when((falling >= 0) & (falling < tiles))
        def _():
            descend(falling)

        @pl.when(t == 0)
        def _():
            a_partial()

        @pl.when(t == 1)
        def _():
            b_partial()

        @pl.when(t == 3)
        def _():
            a_across()

        @pl.when(t == 5)
        def _():
            a_along()

    for j in range(1, n):
        ag_to(j).wait_recv()
    for j in range(1, nd):
        agx_to(j).start()

    for j in range(1, nd):
        b_to(j).wait_recv()
    b_store = pltpu.make_async_copy(b_all, b_out, out_sem.at[0])
    b_store.start()

    @pl.loop(0, tiles)
    def _(t):
        @pl.when(z > 0)
        def _():
            up_to(t, z).wait_recv()
            sums[t, z] = sums[t, z] + from_below[t, z].astype(F32)

        @pl.when(z < n - 1)
        def _():
            down_to(t, z).wait_recv()
            sums[t, z] = sums[t, z] + from_above[t, z].astype(F32)

        dx_out[:, pl.ds(pl.multiple_of(t * TILE, TILE), TILE)] = sums[t, z].astype(BF16)
        pair(t).wait_send()
        for k in range(n):

            @pl.when(k != z)
            def _():
                up_to(t, k).wait_send()

    for j in range(1, nd):
        agx_to(j).wait_recv()
    a_store = pltpu.make_async_copy(a_all, a_out, out_sem.at[1])
    a_store.start()
    a_store.wait()
    b_store.wait()

    proj_copy.wait_send()
    back_copy.wait_send()
    for j in range(1, n):
        proj_z(j).wait_send()
        back_to(j).wait_send()
        az_to(j).wait_send()
        ag_to(j).wait_send()
    for j in range(1, nd):
        b_to(j).wait_send()
        ax_to(j).wait_send()
        agx_to(j).wait_send()


def finish(dx, a_all, b_all, dx_out, ga_out, ua_out, gb_out, ub_out):
    nd, n, a_rows, a_cols = a_all.shape
    rank = ga_out.shape[0]
    dx_out[...] = dx[...]
    for d in range(nd):
        first = d * a_rows
        ref, row = (ga_out, first) if first < rank else (ua_out, first - rank)
        for k in range(n):
            ref[row : row + a_rows, k * a_cols : (k + 1) * a_cols] = a_all[d, k].astype(F32)
    for i, ref in enumerate((gb_out, ub_out)):
        rows = slice(i * rank, (i + 1) * rank)
        total = b_all[0, rows, :].astype(F32)
        for d in range(1, nd):
            total = total + b_all[d, rows, :].astype(F32)
        ref[...] = total


def body(n, nd, tokens, gate, up, hidden_gradient, wg, wu, gd, ud, gu, uu):
    hidden, seq = gate.shape[1:]
    rows, width = tokens.shape[1:]
    rank, half = gd.shape
    tiles = width // TILE
    own = seq // (2 * n)
    a_rows = 2 * rank // nd
    a_cols = half // n
    dma = pltpu.SemaphoreType.DMA
    vmem = pl.BlockSpec(memory_space=pltpu.VMEM)
    hbm = pl.BlockSpec(memory_space=pl.ANY)
    outs = pl.pallas_call(
        functools.partial(kernel, n, nd),
        out_shape=(
            jax.ShapeDtypeStruct((own, width), BF16),
            jax.ShapeDtypeStruct((nd, n, a_rows, a_cols), BF16),
            jax.ShapeDtypeStruct((nd, 2 * rank, hidden), BF16),
        ),
        in_specs=[vmem] + [hbm] * 5 + [vmem] * 4,
        out_specs=(vmem, hbm, hbm),
        scratch_shapes=[
            pltpu.VMEM((hidden, seq), BF16),
            pltpu.VMEM((hidden, seq), BF16),
            pltpu.VMEM((hidden, seq), BF16),
            pltpu.VMEM((seq, hidden), BF16),
            pltpu.VMEM((seq, hidden), BF16),
            pltpu.VMEM((SLOTS, 2, hidden, TILE), BF16),
            pltpu.VMEM((2, seq, TILE), F32),
            pltpu.VMEM((tiles, n, own, TILE), BF16),
            pltpu.VMEM((tiles, n, own, TILE), BF16),
            pltpu.VMEM((tiles, n, own, TILE), F32),
            pltpu.VMEM((tiles, n, own, TILE), BF16),
            pltpu.VMEM((tiles, n, own, TILE), BF16),
            pltpu.VMEM((tiles, n, own, TILE), BF16),
            pltpu.VMEM((2, rows, 2 * rank), F32),
            pltpu.VMEM((n, rows, 2 * rank), BF16),
            pltpu.VMEM((2, seq, 2 * rank), F32),
            pltpu.VMEM((n, rows, 2 * rank), F32),
            pltpu.VMEM((n - 1, rows, 2 * rank), F32),
            pltpu.VMEM((nd, 2 * rank, hidden), BF16),
            pltpu.VMEM((nd, a_rows, half), BF16),
            pltpu.VMEM((nd - 1, a_rows, half), BF16),
            pltpu.VMEM((n, a_rows, a_cols), BF16),
            pltpu.VMEM((n - 1, a_rows, a_cols), BF16),
            pltpu.VMEM((nd, n, a_rows, a_cols), BF16),
            dma((SLOTS, 2)),
            dma((tiles,)),
            dma((tiles,)),
            dma((tiles, n)),
            dma((tiles, n)),
            dma((tiles, n)),
            dma((2,)),
            dma((2,)),
            dma((n - 1,)),
            dma((n - 1,)),
            dma((n - 1,)),
            dma((n - 1,)),
            dma((nd - 1,)),
            dma((nd - 1,)),
            dma((nd - 1,)),
            dma((nd - 1,)),
            dma((n - 1,)),
            dma((n - 1,)),
            dma((n - 1,)),
            dma((n - 1,)),
            dma((nd - 1,)),
            dma((nd - 1,)),
            dma((3,)),
            dma((2,)),
        ],
        compiler_params=pltpu.CompilerParams(
            collective_id=0, has_side_effects=True, vmem_limit_bytes=56 * 1024 * 1024
        ),
        cost_estimate=pl.CostEstimate(
            flops=4 * seq * hidden * width, bytes_accessed=4 * hidden * width, transcendentals=0
        ),
    )(tokens[0], gate[0], up[0], hidden_gradient[0], wg, wu, gd, ud, gu.T, uu.T)
    dx, ga, ua, gb, ub = pl.pallas_call(
        finish,
        out_shape=(
            jax.ShapeDtypeStruct((own, width), BF16),
            jax.ShapeDtypeStruct((rank, half), F32),
            jax.ShapeDtypeStruct((rank, half), F32),
            jax.ShapeDtypeStruct((rank, hidden), F32),
            jax.ShapeDtypeStruct((rank, hidden), F32),
        ),
        in_specs=[vmem] * 3,
        out_specs=(vmem,) * 5,
        compiler_params=pltpu.CompilerParams(vmem_limit_bytes=32 * 1024 * 1024),
    )(*outs)
    return dx[None], ga, ua, gb.T, ub.T


def solution(mesh):
    placed = (
        P(("groups", "dp"), "tensor", None),
        P(("groups", "dp"), ("tensor", "pipe"), None),
        P(("groups", "dp"), ("tensor", "pipe"), None),
        P(("groups", "dp"), ("tensor", "pipe"), None),
        P(("tensor", "pipe"), None),
        P(("tensor", "pipe"), None),
        P(None, "pipe"),
        P(None, "pipe"),
        P(("tensor", "pipe"), None),
        P(("tensor", "pipe"), None),
    )
    return jax.shard_map(
        functools.partial(body, mesh.shape["tensor"], mesh.shape["dp"]),
        mesh=mesh,
        in_specs=placed,
        out_specs=(
            P(("groups", "dp"), ("tensor", "pipe"), None),
            P("groups", "pipe"),
            P("groups", "pipe"),
            P(("groups", "tensor", "pipe"), None),
            P(("groups", "tensor", "pipe"), None),
        ),
        check_vma=False,
    )
```
